256 devices in a mesh: ctx: 16 (over x, z_hi), head: 16 (over y, z_lo, core).
Axes of the slice: x: 4, y: 4, z: 8 (z_hi: 4, z_lo: 2; z = z_hi * 2 + z_lo), core: 2. Of those that a mesh axis runs over, the one named last changes fastest.
Arguments:
- queries: bfloat16 [16384, 4096], P(('ctx', 'head')), may hold values from -200 to 200
- keys: bfloat16 [16384, 512], P(('ctx', 'head')), may hold values from -6 to 6
- values: bfloat16 [16384, 512], P(('ctx', 'head')), may hold values from -6 to 6
Outputs:
- attended: bfloat16 [16384, 4096], P(('ctx', 'head'))
The draws below stay inside these ranges and needn't reach their ends.
All inputs are finite; a program needn't handle non-finite values.
Results may differ from the reference program's by a relative error of at most 0.0065.
Values may be sent and summed in bfloat16 or wider, within the bound.
A program may use at most 64 MiB of HBM per device.

```python
import math
import jax
import jax.numpy as jnp
from jax import lax

QH = 32
KVH = 4
HD = 128
TOKENS = 16384


def base_keys(key):
    return jnp.clip(jax.random.normal(key, (TOKENS, KVH, HD), jnp.float32), -6.0, 6.0)


def draw_keys(key, part):
    shared = base_keys(key)
    return shared.reshape(TOKENS, KVH * HD).astype(jnp.bfloat16)


def draw_queries(key, part):
    key = jax.random.fold_in(key, 7)
    own = jnp.clip(jax.random.normal(key, (TOKENS, QH, HD), jnp.float32), -6.0, 6.0)
    return own.reshape(TOKENS, QH * HD).astype(jnp.bfloat16)


def block_scale(rng, shape, pieces, least, top_value):
    gain = 1.0
    for axis_at, shards_of in pieces:
        steps = jax.random.uniform(jax.random.fold_in(jax.random.fold_in(rng, 6), axis_at), (shards_of,), jnp.float32, least / len(pieces), top_value / len(pieces))
        gain = gain * jnp.repeat(jnp.exp(steps), shape[axis_at] // shards_of).reshape((-1,) + (1,) * (len(shape) - 1 - axis_at))
    return gain


def normal_values(stream_key, extent, width, limit, cuts=(), held_as=jnp.bfloat16):
    values = width * jax.random.normal(stream_key, extent, jnp.float32)
    if cuts:
        values = values * block_scale(stream_key, extent, cuts, -0.22, 0.18)
    return jnp.clip(values, -limit, limit).astype(held_as)


def setup_inputs(seed: int = 0) -> dict:
    seeds = jax.random.split(jax.random.key(seed), 4)
    queries = draw_queries(jax.random.fold_in(seeds[3], 71), 0)
    keys = draw_keys(jax.random.fold_in(seeds[3], 71), 0)
    values = normal_values(seeds[2], (TOKENS, KVH * HD), 1.0, 6.0, ((0, 256),))
    return {"queries": queries, "keys": keys, "values": values}


def reference(queries, keys, values):
    group = QH // KVH
    scale = 1.0 / math.sqrt(HD)
    query_all = queries.reshape(TOKENS, KVH, group, HD).transpose(1, 0, 2, 3)
    key_all = keys.reshape(TOKENS, KVH, HD).transpose(1, 0, 2)
    value_all = values.reshape(TOKENS, KVH, HD).transpose(1, 0, 2)
    block = math.gcd(TOKENS, 1024)
    count = TOKENS // block
    key_pos = jnp.arange(TOKENS, dtype=jnp.int32)

    def per_head(inputs):
        query_head, key_head, value_head = inputs
        key_float = key_head.astype(jnp.float32)
        value_float = value_head.astype(jnp.float32)

        def per_block(index):
            first = (index * block).astype(jnp.int32)
            query_rows = lax.dynamic_slice_in_dim(query_head, first, block, 0).astype(jnp.float32)
            scores = jnp.einsum('tgd,kd->gtk', query_rows, key_float) * scale
            query_pos = first + jnp.arange(block, dtype=jnp.int32)
            allowed = query_pos[:, None] >= key_pos[None, :]
            scores = jnp.where(allowed, scores, -1e+30)
            peak = lax.optimization_barrier(jnp.max(scores, axis=-1, keepdims=True))
            weights = jnp.exp(scores - peak)
            totals = lax.optimization_barrier(jnp.sum(weights, axis=-1))
            rounded = lax.optimization_barrier(weights.astype(jnp.bfloat16)).astype(jnp.float32)
            summed = jnp.einsum('gtk,kd->tgd', rounded, value_float)
            return (summed / totals.T[:, :, None]).astype(jnp.bfloat16)
        return lax.map(per_block, jnp.arange(count, dtype=jnp.int32))
    outputs = lax.map(per_head, (query_all, key_all, value_all))
    return outputs.transpose(1, 2, 0, 3, 4).reshape(TOKENS, QH * HD)
```

```python
import functools
import math

import jax
import jax.numpy as jnp
from jax import lax
from jax.experimental import pallas as pl
from jax.experimental.pallas import tpu as pltpu
from jax.sharding import PartitionSpec as P

QH = 32
KVH = 4
HD = 128
GROUP = QH // KVH
NX, NY, NZ = 4, 4, 8
TOK = 64
ROWS = TOK * GROUP
SPAN = TOK * NY * 2
WIDE = GROUP * HD
TILE = 256
SCALE = math.log2(math.e) / math.sqrt(HD)
LOW = -1e30
MESH = pl.DeviceIdType.MESH


def mod(a, n):
    return lax.rem(a + n, n)


def device(x, y, z, c):
    return (x * 4 + z // 2, y * 4 + lax.rem(z, 2) * 2 + c)


def offset(n):
    d = (n + 1) // 2
    return d * (1 - 2 * lax.rem(n, 2))


def kernel(
    q_hbm, k_hbm, v_hbm, o_hbm,
    kv, qb, ob, q2, m_ref, acc,
    own_sem, qs_sem, qr_sem, ks_sem, kr_sem, os_sem, or_sem,
    piece_recv, sib_send, ring_send, aux_send,
):
    ctx, head = lax.axis_index("ctx"), lax.axis_index("head")
    x, zh = ctx // 4, lax.rem(ctx, 4)
    y, zl, c = head // 4, lax.rem(head, 4) // 2, lax.rem(head, 2)
    z = zh * 2 + zl
    sibling = device(x, y, z, 1 - c)
    z_next, z_prev = device(x, y, mod(z + 1, NZ), c), device(x, y, mod(z - 1, NZ), c)
    y_next, y_prev = device(x, mod(y + 1, NY), z, c), device(x, mod(y - 1, NY), z, c)
    y_far = device(x, mod(y + 2, NY), z, c)
    x_peers = [device(mod(x + i, NX), y, z, c) for i in (1, 2, 3)]

    barrier = pltpu.get_barrier_semaphore()
    peers = [sibling, z_next, z_prev, y_next, y_prev, y_far] + x_peers
    for peer in peers:
        pl.semaphore_signal(barrier, inc=1, device_id=peer, device_id_type=MESH)
    pl.semaphore_wait(barrier, len(peers))

    def part(yy, cc):
        return pl.ds(pl.multiple_of((yy * 2 + cc) * TOK, TOK), TOK)

    def columns(i, width):
        return pl.ds(pl.multiple_of(i * width, width), width)

    mine = part(y, c)

    def kv_copy(i, which, owner):
        peer_x = mod(x + i, NX)
        ref = (k_hbm, v_hbm)[which]
        return pltpu.make_async_remote_copy(
            src_ref=ref.at[:, columns(peer_x, HD)],
            dst_ref=kv.at[z, owner, mine, pl.ds(which * HD, HD)],
            send_sem=ks_sem.at[i, which],
            recv_sem=kr_sem.at[owner, which],
            device_id=x_peers[i - 1],
            device_id_type=MESH,
        )

    def q_copy(i, owner):
        return pltpu.make_async_remote_copy(
            src_ref=q_hbm.at[:, columns(mod(x + i, NX), WIDE)],
            dst_ref=qb.at[owner],
            send_sem=qs_sem.at[i],
            recv_sem=qr_sem.at[owner],
            device_id=x_peers[i - 1],
            device_id_type=MESH,
        )

    def o_copy(i, owner):
        return pltpu.make_async_remote_copy(
            src_ref=ob.at[mod(x + i, NX)],
            dst_ref=o_hbm.at[:, columns(owner, WIDE)],
            send_sem=os_sem.at[i],
            recv_sem=or_sem.at[owner],
            device_id=x_peers[i - 1],
            device_id_type=MESH,
        )

    own_k = pltpu.make_async_copy(
        k_hbm.at[:, columns(x, HD)], kv.at[z, x, mine, pl.ds(0, HD)], own_sem.at[0])
    own_v = pltpu.make_async_copy(
        v_hbm.at[:, columns(x, HD)], kv.at[z, x, mine, pl.ds(HD, HD)], own_sem.at[1])
    own_q = pltpu.make_async_copy(q_hbm.at[:, columns(x, WIDE)], qb.at[x], own_sem.at[2])
    own_o = pltpu.make_async_copy(ob.at[x], o_hbm.at[:, columns(x, WIDE)], own_sem.at[3])

    def piece(zz, yy, cc, peer, send):
        ref = kv.at[zz, :, part(yy, cc), :]
        return pltpu.make_async_remote_copy(
            src_ref=ref, dst_ref=ref, send_sem=send, recv_sem=piece_recv.at[zz, yy, cc],
            device_id=peer, device_id_type=MESH,
        )

    def place(n):
        return mod(z + offset(n), NZ), (n + 1) // 2, lax.rem(n, 2) == 1

    def sends0(n, k, act):
        zz, far, up = place(n)
        def to(peer, sem):
            act(piece(zz, k, 0, peer, sem))
        to_next = (n == 0) | (up & ((far < 3) | ((far == 3) & (k < 2))))
        to_prev = (n == 0) | (~up & ((far < 3) | ((far == 3) & (k >= 2))))
        pl.when(to_next)(lambda: to(z_next, ring_send.at[n, k, 0]))
        pl.when(to_prev)(lambda: to(z_prev, ring_send.at[n, k, 1]))
        to(sibling, sib_send.at[n, k])

    def sends1(n, k, act):
        zz, far, up = place(n)
        yy = mod(y + (0, -1, 1, 2)[k], NY)
        def to(peer, sem):
            act(piece(zz, yy, 1, peer, sem))
        if k == 0:
            even = lax.rem(y, 2) == 0
            to_next = (n == 0) | (up & ((far < 3) | ((far == 3) & even)))
            to_prev = (n == 0) | (~up & ((far < 3) | ((far == 3) & ~even)))
            pl.when(to_next)(lambda: to(z_next, aux_send.at[n, 0]))
            pl.when(to_prev)(lambda: to(z_prev, aux_send.at[n, 1]))
            to(y_next, ring_send.at[n, k, 0])
            to(y_prev, ring_send.at[n, k, 1])
        if k == 1:
            pl.when(lax.rem(zz, 2) == 0)(lambda: to(y_next, ring_send.at[n, k, 0]))
        if k == 2:
            pl.when(lax.rem(zz, 2) == 1)(lambda: to(y_prev, ring_send.at[n, k, 1]))
        to(sibling, sib_send.at[n, k])

    def await_piece(n, yy, cc):
        piece(place(n)[0], yy, cc, sibling, sib_send.at[n, 0]).wait_recv()

    def start(copy):
        copy.start()

    def sent(copy):
        copy.wait_send()

    def serve0(n, k):
        await_piece(n, k, 0)
        sends0(n, k, start)

    def serve1(n, k):
        await_piece(n, mod(y + (0, -1, 1, 2)[k], NY), 1)
        sends1(n, k, start)

    def far_sends(act):
        @pl.when(c == 0)
        def _():
            for i, peer in enumerate((y_next, y_prev, y_far)):
                act(piece(z, y, 0, peer, aux_send.at[i, 0]))

    for i in (1, 2, 3):
        for which in (0, 1):
            kv_copy(i, which, x).start()
    own_k.start()
    own_v.start()
    for i in (1, 2, 3):
        q_copy(i, x).start()
    own_q.start()
    own_k.wait()
    own_v.wait()
    for i in (1, 2, 3):
        for which in (0, 1):
            kv_copy(i, which, mod(x - i, NX)).wait_recv()
    far_sends(start)

    m_ref[...] = jnp.full_like(m_ref, LOW)
    acc[...] = jnp.zeros_like(acc)

    @pl.when(c == 0)
    def _():
        sends0(0, y, start)
        def others(i, _):
            serve0(0, mod(y + i, NY))
            return 0
        lax.fori_loop(1, NY, others, 0)
        lax.fori_loop(0, NY, lambda k, _: (serve0(1, k), 0)[1], 0)

    @pl.when(c == 1)
    def _():
        sends1(0, 0, start)
        serve1(1, 0)
        serve1(0, 1)
        serve1(0, 2)
        serve1(2, 0)
        serve1(1, 1)
        serve1(1, 2)
        serve1(0, 3)

    own_q.wait()
    for i in (1, 2, 3):
        q_copy(i, mod(x - i, NX)).wait_recv()

    def prepare(r, _):
        for g in range(GROUP):
            full = qb[r, :, g * HD:(g + 1) * HD].astype(jnp.float32) * SCALE
            high = full.astype(jnp.bfloat16)
            rows = pl.ds(pl.multiple_of(r * ROWS + g * TOK, TOK), TOK)
            q2[rows, :HD] = high
            q2[rows, HD:] = (full - high.astype(jnp.float32)).astype(jnp.bfloat16)
        return 0

    lax.fori_loop(0, NX, prepare, 0)

    def attend(zz, r, diagonal):
        spans = r + 1 if diagonal else r
        if not spans:
            return
        keys = kv[zz, :spans, :, :HD].reshape(spans * SPAN, HD)
        values = kv[zz, :spans, :, HD:].reshape(spans * SPAN, HD)
        keys = jnp.concatenate([keys, keys], axis=1)
        values = jnp.concatenate([values, jnp.ones_like(values)], axis=1)
        tiles = [pl.ds(r * ROWS + i * TILE, TILE) for i in range(ROWS // TILE)]
        scores = [
            lax.dot_general(
                q2[t, :], keys, (((1,), (1,)), ((), ())), preferred_element_type=jnp.float32)
            for t in tiles
        ]
        old = [m_ref[t, :] for t in tiles]
        sums = [acc[t, :] for t in tiles]
        if diagonal:
            lane = lax.broadcasted_iota(jnp.int32, (TILE, HD), 1)
            row = lax.rem(lax.broadcasted_iota(jnp.int32, (TILE, HD), 0), TOK)
            ahead = lane - row
            span_gap = (zh - zz // 2) * (2 * SPAN) + head * TOK - lax.rem(zz, 2) * 2 * TOK
        done = []
        for score, peak, total in zip(scores, old, sums):
            cols = [score[:, j * HD:(j + 1) * HD] for j in range(spans * SPAN // HD)]
            if diagonal:
                for j in range(SPAN // HD):
                    at = len(cols) - SPAN // HD + j
                    cols[at] = jnp.where(ahead <= span_gap - j * 4 * TOK, cols[at], LOW)
            top = cols
            while len(top) > 1:
                rest = top[len(top) // 2 * 2:]
                top = [jnp.maximum(a, b) for a, b in zip(top[::2], top[1::2])] + rest
            top = jnp.maximum(peak, jnp.max(top[0], axis=1, keepdims=True))
            factor = jnp.exp2(peak - top)
            weights = jnp.concatenate(
                [jnp.exp2(col - top).astype(jnp.bfloat16) for col in cols], axis=1)
            added = jnp.dot(weights, values, preferred_element_type=jnp.float32)
            total = jnp.concatenate([total[:, :HD] * factor, total[:, HD:] * factor], axis=1)
            done.append((total + added, top))
        for t, (total, top) in zip(tiles, done):
            acc[t, :] = total
            m_ref[t, :] = top

    def block(n, _):
        zz = mod(z + offset(n), NZ)
        lax.fori_loop(0, NY, lambda k, _: (await_piece(n, k, 1 - c), 0)[1], 0)
        for slot, r in enumerate((3, 2, 1, 0)):
            ahead = (3, 2, 2, 1)[slot]
            pl.when((c == 0) & (n + 2 < NZ))(lambda: serve0(n + 2, slot))
            pl.when((c == 1) & (n + ahead < NZ))(lambda: serve1(n + ahead, slot))
            inside = zz // 2 <= zh
            pl.when(inside)(lambda: attend(zz, r, True))
            pl.when(~inside)(lambda: attend(zz, r, False))
        return 0

    lax.fori_loop(0, NZ, block, 0)

    def finish(r):
        for g in range(GROUP):
            rows = pl.ds(pl.multiple_of(r * ROWS + g * TOK, TOK), TOK)
            out = acc[rows, :HD] / acc[rows, HD:]
            ob[r, :, g * HD:(g + 1) * HD] = out.astype(jnp.bfloat16)

    for i in (2, 1, 3):
        finish(mod(x + i, NX))
        o_copy(i, x).start()
    finish(x)
    own_o.start()

    for i in (1, 2, 3):
        for which in (0, 1):
            kv_copy(i, which, x).wait_send()
        q_copy(i, x).wait_send()
    far_sends(sent)
    def drain(n, _):
        for k in range(4):
            pl.when(c == 0)(lambda: sends0(n, k, sent))
            pl.when(c == 1)(lambda: sends1(n, k, sent))
        return 0
    lax.fori_loop(0, NZ, drain, 0)
    own_o.wait()
    for i in (1, 2, 3):
        o_copy(i, x).wait_send()
        o_copy(i, mod(x - i, NX)).wait_recv()


def shards(queries, keys, values):
    dma = pltpu.SemaphoreType.DMA
    return pl.pallas_call(
        kernel,
        out_shape=jax.ShapeDtypeStruct(queries.shape, jnp.bfloat16),
        in_specs=[pl.BlockSpec(memory_space=pl.ANY)] * 3,
        out_specs=pl.BlockSpec(memory_space=pl.ANY),
        scratch_shapes=[
            pltpu.VMEM((NZ, NX, SPAN, 2 * HD), jnp.bfloat16),
            pltpu.VMEM((NX, TOK, WIDE), jnp.bfloat16),
            pltpu.VMEM((NX, TOK, WIDE), jnp.bfloat16),
            pltpu.VMEM((NX * ROWS, 2 * HD), jnp.bfloat16),
            pltpu.VMEM((NX * ROWS, HD), jnp.float32),
            pltpu.VMEM((NX * ROWS, 2 * HD), jnp.float32),
            dma((4,)), dma((4,)), dma((4,)), dma((4, 2)), dma((4, 2)), dma((4,)), dma((4,)),
            dma((NZ, NY, 2)), dma((NZ, 4)), dma((NZ, 4, 2)), dma((NZ, 2)),
        ],
        compiler_params=pltpu.CompilerParams(
            collective_id=0, has_side_effects=True, vmem_limit_bytes=56 << 20),
        cost_estimate=pl.CostEstimate(
            flops=9 << 30, bytes_accessed=2 << 20, transcendentals=17 << 20),
    )(queries, keys, values)


def solution(mesh):
    spec = P(("ctx", "head"), None)
    return jax.shard_map(
        shards, mesh=mesh, in_specs=(spec, spec, spec), out_specs=spec, check_vma=False)
```

```python
import functools
import math

import jax
import jax.numpy as jnp
from jax import lax
from jax.experimental import pallas as pl
from jax.experimental.pallas import tpu as pltpu
from jax.sharding import PartitionSpec as P

QH = 32
KVH = 4
HD = 128
GROUP = QH // KVH
NX, NY, NZ = 4, 4, 8
TOK = 64
ROWS = TOK * GROUP
SPAN = TOK * NY * 2
WIDE = GROUP * HD
TILE = 256
SCALE = math.log2(math.e) / math.sqrt(HD)
LOW = -1e30
HELD = 2
MESH = pl.DeviceIdType.MESH


def mod(a, n):
    return lax.rem(a + n, n)


def device(x, y, z, c):
    return (x * 4 + z // 2, y * 4 + lax.rem(z, 2) * 2 + c)


def offset(n):
    d = (n + 1) // 2
    return d * (1 - 2 * lax.rem(n, 2))


def kernel(
    q_hbm, k_hbm, v_hbm, o_hbm,
    kv, qb, ob, m_ref, acc,
    own_sem, qs_sem, qr_sem, ks_sem, kr_sem, os_sem, or_sem,
    piece_recv, sib_recv, sib_send, ring_send, aux_send,
):
    ctx, head = lax.axis_index("ctx"), lax.axis_index("head")
    x, zh = ctx // 4, lax.rem(ctx, 4)
    y, zl, c = head // 4, lax.rem(head, 4) // 2, lax.rem(head, 2)
    z = zh * 2 + zl
    sibling = device(x, y, z, 1 - c)
    z_next, z_prev = device(x, y, mod(z + 1, NZ), c), device(x, y, mod(z - 1, NZ), c)
    y_next, y_prev = device(x, mod(y + 1, NY), z, c), device(x, mod(y - 1, NY), z, c)
    y_far = device(x, mod(y + 2, NY), z, c)
    x_peers = [device(mod(x + i, NX), y, z, c) for i in (1, 2, 3)]

    barrier = pltpu.get_barrier_semaphore()
    peers = [sibling, z_next, z_prev, y_next, y_prev, y_far] + x_peers
    for peer in peers:
        pl.semaphore_signal(barrier, inc=1, device_id=peer, device_id_type=MESH)
    pl.semaphore_wait(barrier, len(peers))

    def part(yy, cc):
        return pl.ds(pl.multiple_of((cc * NY + yy) * TOK, TOK), TOK)

    def columns(i, width):
        return pl.ds(pl.multiple_of(i * width, width), width)

    mine = part(y, c)

    def kv_copy(i, which, owner):
        peer_x = mod(x + i, NX)
        ref = (k_hbm, v_hbm)[which]
        return pltpu.make_async_remote_copy(
            src_ref=ref.at[:, columns(peer_x, HD)],
            dst_ref=kv.at[z, owner, mine, pl.ds(which * HD, HD)],
            send_sem=ks_sem.at[i, which],
            recv_sem=kr_sem.at[owner, which],
            device_id=x_peers[i - 1],
            device_id_type=MESH,
        )

    def q_copy(i):
        return pltpu.make_async_remote_copy(
            src_ref=q_hbm.at[:, columns(mod(x + i, NX), WIDE)],
            dst_ref=qb.at[x],
            send_sem=qs_sem.at[i],
            recv_sem=qr_sem.at[x],
            device_id=x_peers[i - 1],
            device_id_type=MESH,
        )

    def q_arrival(r):
        return pltpu.make_async_remote_copy(
            src_ref=qb.at[r], dst_ref=qb.at[r], send_sem=qs_sem.at[0], recv_sem=qr_sem.at[r],
            device_id=sibling, device_id_type=MESH,
        )

    def o_copy(r, owner):
        return pltpu.make_async_remote_copy(
            src_ref=ob.at[r],
            dst_ref=o_hbm.at[:, columns(owner, WIDE)],
            send_sem=os_sem.at[r],
            recv_sem=or_sem.at[owner],
            device_id=device(r, y, z, c),
            device_id_type=MESH,
        )

    own_k = pltpu.make_async_copy(
        k_hbm.at[:, columns(x, HD)], kv.at[z, x, mine, pl.ds(0, HD)], own_sem.at[0])
    own_v = pltpu.make_async_copy(
        v_hbm.at[:, columns(x, HD)], kv.at[z, x, mine, pl.ds(HD, HD)], own_sem.at[1])
    own_q = pltpu.make_async_copy(q_hbm.at[:, columns(x, WIDE)], qb.at[x], own_sem.at[2])
    own_o = pltpu.make_async_copy(ob.at[x], o_hbm.at[:, columns(x, WIDE)], own_sem.at[3])

    def piece(zz, yy, cc, peer, send):
        ref = kv.at[zz, :, part(yy, cc), :]
        return pltpu.make_async_remote_copy(
            src_ref=ref, dst_ref=ref, send_sem=send, recv_sem=piece_recv.at[zz, yy, cc],
            device_id=peer, device_id_type=MESH,
        )

    def half(zz, n, cc):
        ref = kv.at[zz, :, pl.ds(pl.multiple_of(cc * NY * TOK, NY * TOK), NY * TOK), :]
        return pltpu.make_async_remote_copy(
            src_ref=ref, dst_ref=ref, send_sem=sib_send.at[n, 0], recv_sem=sib_recv.at[n],
            device_id=sibling, device_id_type=MESH,
        )

    def to_sibling(n, k, cc, act):
        zz = place(n)[0]
        def one():
            act(piece(zz, mod(y + offset(k), NY), cc, sibling, sib_send.at[0, k]))
        pl.when(n == 0)(one)
        pl.when((n > 0) & (k == NY - 1))(lambda: act(half(zz, n, cc)))

    def await_sibling(n):
        def pieces():
            for k in range(NY):
                await_piece(0, k, 1 - c)
        pl.when(n == 0)(pieces)
        pl.when(n > 0)(lambda: half(place(n)[0], n, 1 - c).wait_recv())

    def place(n):
        return mod(z + offset(n), NZ), (n + 1) // 2, lax.rem(n, 2) == 1

    def sends0(n, k, act):
        zz, far, up = place(n)
        def to(peer, sem):
            act(piece(zz, mod(y + offset(k), NY), 0, peer, sem))
        to_sibling(n, k, 0, act)
        to_next = (n == 0) | (up & ((far < 3) | ((far == 3) & (k < 2))))
        to_prev = (n == 0) | (~up & ((far < 3) | ((far == 3) & (k >= 2))))
        pl.when(to_next)(lambda: to(z_next, ring_send.at[n, k, 0]))
        pl.when(to_prev)(lambda: to(z_prev, ring_send.at[n, k, 1]))

    def sends1(n, k, act):
        zz, far, up = place(n)
        def to(peer, sem):
            act(piece(zz, mod(y + offset(k), NY), 1, peer, sem))
        to_sibling(n, k, 1, act)
        if k == 0:
            even = lax.rem(y, 2) == 0
            to_next = (n == 0) | (up & ((far < 3) | ((far == 3) & even)))
            to_prev = (n == 0) | (~up & ((far < 3) | ((far == 3) & ~even)))
            pl.when(to_next)(lambda: to(z_next, ring_send.at[n, 3, 0]))
            pl.when(to_prev)(lambda: to(z_prev, ring_send.at[n, 3, 1]))

    def along_y(n, cc, act):
        for i, peer in enumerate((y_next, y_prev, y_far)):
            act(piece(place(n)[0], y, cc, peer, aux_send.at[n, i]))

    def await_piece(n, k, cc):
        yy = mod(y + offset(k), NY)
        piece(place(n)[0], yy, cc, sibling, sib_send.at[n, k]).wait_recv()

    def start(copy):
        copy.start()

    def sent(copy):
        copy.wait_send()

    def serve0(n, k):
        await_piece(n, k, 0)
        sends0(n, k, start)

    def relay1(n, k):
        await_piece(n, k, 1)
        to_sibling(n, k, 1, start)

    def serve1(n, k):
        await_piece(n, k, 1)
        sends1(n, k, start)
        if k == 0:
            if n >= HELD:
                along_y(n - HELD, 1, sent)
            along_y(n, 1, start)

    def pair0(d, k):
        serve0(2 * d - 1, k)
        serve0(2 * d, k)

    for i in (1, 2, 3):
        for which in (0, 1):
            kv_copy(i, which, x).start()
    own_k.start()
    own_v.start()
    for i in (1, 3):
        q_copy(i).start()
    own_q.start()
    own_k.wait()
    own_v.wait()
    for i in (1, 2, 3):
        for which in (0, 1):
            kv_copy(i, which, mod(x - i, NX)).wait_recv()

    @pl.when(c == 0)
    def _():
        sends0(0, 0, start)
        along_y(0, 0, start)

    @pl.when(c == 1)
    def _():
        sends1(0, 0, start)
        along_y(0, 1, start)

    q_copy(2).start()
    m_ref[...] = jnp.full_like(m_ref, LOW)
    acc[...] = jnp.zeros_like(acc)

    @pl.when(c == 0)
    def _():
        lax.fori_loop(1, NY, lambda k, _: (serve0(0, k), 0)[1], 0)

    @pl.when(c == 1)
    def _():
        lax.fori_loop(1, NY, lambda k, _: (relay1(0, k), 0)[1], 0)
        serve1(1, 0)
        serve1(2, 0)

    def attend(zz, r, diagonal):
        spans = r + 1 if diagonal else r
        if not spans:
            return
        keys = kv[zz, :spans, :, :HD].reshape(spans * SPAN, HD)
        values = kv[zz, :spans, :, HD:].reshape(spans * SPAN, HD)
        values = jnp.concatenate([values, jnp.ones_like(values)], axis=1)
        tiles = [pl.ds(r * ROWS + i * TILE, TILE) for i in range(ROWS // TILE)]
        scores = []
        for i in range(len(tiles)):
            heads = range(i * TILE // TOK, (i + 1) * TILE // TOK)
            query = jnp.concatenate([qb[r, :, g * HD:(g + 1) * HD] for g in heads], axis=0)
            scores.append(lax.dot_general(
                query, keys, (((1,), (1,)), ((), ())), preferred_element_type=jnp.float32))
        old = [m_ref[t, :] for t in tiles]
        sums = [acc[t, :] for t in tiles]
        if diagonal:
            lane = lax.broadcasted_iota(jnp.int32, (TILE, HD), 1)
            row = lax.rem(lax.broadcasted_iota(jnp.int32, (TILE, HD), 0), TOK)
            ahead = lane // TOK * (4 * TOK) + lax.rem(lane, TOK) - row
            span_gap = (zh - zz // 2) * (2 * SPAN) + head * TOK - lax.rem(zz, 2) * 2 * TOK
        done = []
        for score, peak, total in zip(scores, old, sums):
            cols = [score[:, j * HD:(j + 1) * HD] for j in range(spans * SPAN // HD)]
            if diagonal:
                for j in range(SPAN // HD):
                    at = len(cols) - SPAN // HD + j
                    cols[at] = jnp.where(
                        ahead <= span_gap - (j % 2 * 8 + j // 2) * TOK, cols[at], LOW)
            top = cols
            while len(top) > 1:
                rest = top[len(top) // 2 * 2:]
                top = [jnp.maximum(a, b) for a, b in zip(top[::2], top[1::2])] + rest
            top = jnp.maximum(peak, jnp.max(top[0], axis=1, keepdims=True))
            factor = jnp.exp2((peak - top) * SCALE)
            weights = jnp.concatenate(
                [jnp.exp2((col - top) * SCALE).astype(jnp.bfloat16) for col in cols], axis=1)
            added = jnp.dot(weights, values, preferred_element_type=jnp.float32)
            total = jnp.concatenate([total[:, :HD] * factor, total[:, HD:] * factor], axis=1)
            done.append((total + added, top))
        for t, (total, top) in zip(tiles, done):
            acc[t, :] = total
            m_ref[t, :] = top

    def finish(r):
        for g in range(GROUP):
            rows = pl.ds(pl.multiple_of(r * ROWS + g * TOK, TOK), TOK)
            out = acc[rows, :HD] / acc[rows, HD:]
            ob[r, :, g * HD:(g + 1) * HD] = out.astype(jnp.bfloat16)

    def work(w, _):
        last = w >= 4 * (NZ - 2)
        slot = jnp.where(last, (w - 4 * (NZ - 2)) // 2, lax.rem(w, 4))
        n = jnp.where(last, NZ - 2 + lax.rem(w, 2), w // 4)
        near = slot + jnp.where(slot == 2, 1, 0) - jnp.where(slot == 3, 1, 0)
        turn = lax.rem(x + jnp.where(last, slot + 1, near), NX)
        r = jnp.where(last | (n == 0), turn, 3 - slot)
        zz = mod(z + offset(n), NZ)

        @pl.when(jnp.where(last, w < 4 * (NZ - 2) + 2, slot == 0))
        def _():
            await_sibling(n)

        @pl.when((c == 0) & (n < 6))
        def _():
            @pl.when((n == 0) & (slot > 0))
            def _():
                pair0(1, slot - 1)
                pl.when(slot == 3)(lambda: pair0(1, 3))

            @pl.when((n > 0) & (n < 5))
            def _():
                far = (n - 1) // 2 + 2
                serve0(2 * far - 1 + lax.rem(slot, 2), 2 * lax.rem(n + 1, 2) + slot // 2)

            @pl.when((n == 5) & (slot > 1))
            def _():
                serve0(7, slot - 2)
                serve0(7, slot)

        @pl.when((c == 1) & (n < 6))
        def _():
            for at, at_slot, m in ((0, 1, 3), (0, 2, 4), (1, 0, 5), (1, 1, 6), (2, 0, 7)):
                pl.when((n == at) & (slot == at_slot))(lambda: serve1(m, 0))
            pl.when(slot > 0)(lambda: relay1(n + 1, slot))

            @pl.when((n == 5) & (slot == 3))
            def _():
                lax.fori_loop(1, NY, lambda k, _: (relay1(7, k), 0)[1], 0)

        @pl.when(n == 0)
        def _():
            pl.when(r == x)(own_q.wait)
            pl.when(r != x)(lambda: q_arrival(r).wait_recv())

        for quarter in range(NX):
            inside = zz // 2 <= zh
            pl.when((r == quarter) & inside)(lambda: attend(zz, quarter, True))
            pl.when((r == quarter) & ~inside)(lambda: attend(zz, quarter, False))

        @pl.when(last & (lax.rem(w, 2) == 1))
        def _():
            finish(r)
            pl.when(r != x)(lambda: o_copy(r, x).start())
            pl.when(r == x)(own_o.start)
        return 0

    lax.fori_loop(0, 4 * NZ, work, 0)

    for i in (1, 2, 3):
        for which in (0, 1):
            kv_copy(i, which, x).wait_send()
        q_copy(i).wait_send()
    pl.when(c == 0)(lambda: along_y(0, 0, sent))

    @pl.when(c == 1)
    def _():
        for n in range(NZ - HELD, NZ):
            along_y(n, 1, sent)

    def drain(n, _):
        for k in range(4):
            pl.when(c == 0)(lambda: sends0(n, k, sent))
            pl.when(c == 1)(lambda: sends1(n, k, sent))
        return 0

    lax.fori_loop(0, NZ, drain, 0)
    own_o.wait()
    for r in range(NX):
        pl.when(r != x)(lambda: o_copy(r, x).wait_send())
        pl.when(r != x)(lambda: o_copy(r, r).wait_recv())


def shards(queries, keys, values):
    dma = pltpu.SemaphoreType.DMA
    return pl.pallas_call(
        kernel,
        out_shape=jax.ShapeDtypeStruct(queries.shape, jnp.bfloat16),
        in_specs=[pl.BlockSpec(memory_space=pl.ANY)] * 3,
        out_specs=pl.BlockSpec(memory_space=pl.ANY),
        scratch_shapes=[
            pltpu.VMEM((NZ, NX, SPAN, 2 * HD), jnp.bfloat16),
            pltpu.VMEM((NX, TOK, WIDE), jnp.bfloat16),
            pltpu.VMEM((NX, TOK, WIDE), jnp.bfloat16),
            pltpu.VMEM((NX * ROWS, HD), jnp.float32),
            pltpu.VMEM((NX * ROWS, 2 * HD), jnp.float32),
            dma((4,)), dma((4,)), dma((4,)), dma((4, 2)), dma((4, 2)), dma((4,)), dma((4,)),
            dma((NZ, NY, 2)), dma((NZ,)), dma((NZ, 4)), dma((NZ, 4, 2)), dma((NZ, 3)),
        ],
        compiler_params=pltpu.CompilerParams(
            collective_id=0, has_side_effects=True, vmem_limit_bytes=56 << 20),
        cost_estimate=pl.CostEstimate(
            flops=9 << 30, bytes_accessed=2 << 20, transcendentals=17 << 20),
    )(queries, keys, values)


def solution(mesh):
    spec = P(("ctx", "head"), None)
    return jax.shard_map(
        shards, mesh=mesh, in_specs=(spec, spec, spec), out_specs=spec, check_vma=False)
```

```python
import functools
import math

import jax
import jax.numpy as jnp
from jax import lax
from jax.experimental import pallas as pl
from jax.experimental.pallas import tpu as pltpu
from jax.sharding import PartitionSpec as P

QH = 32
KVH = 4
HD = 128
GROUP = QH // KVH
NX, NY, NZ = 4, 4, 8
TOK = 64
ROWS = TOK * GROUP
SPAN = TOK * NY * 2
WIDE = GROUP * HD
TILE = 256
SCALE = math.log2(math.e) / math.sqrt(HD)
LOW = -1e30
HELD = 2
MESH = pl.DeviceIdType.MESH


def mod(a, n):
    return lax.rem(a + n, n)


def device(x, y, z, c):
    return (x * 4 + z // 2, y * 4 + lax.rem(z, 2) * 2 + c)


def offset(n):
    d = (n + 1) // 2
    return d * (1 - 2 * lax.rem(n, 2))


def kernel(
    q_hbm, k_hbm, v_hbm, o_hbm,
    kv, qb, ob, m_ref, acc,
    own_sem, qs_sem, qr_sem, ks_sem, kr_sem, os_sem, or_sem,
    piece_recv, sib_recv, sib_send, ring_send, aux_send,
):
    ctx, head = lax.axis_index("ctx"), lax.axis_index("head")
    x, zh = ctx // 4, lax.rem(ctx, 4)
    y, zl, c = head // 4, lax.rem(head, 4) // 2, lax.rem(head, 2)
    z = zh * 2 + zl
    sibling = device(x, y, z, 1 - c)
    z_next, z_prev = device(x, y, mod(z + 1, NZ), c), device(x, y, mod(z - 1, NZ), c)
    y_next, y_prev = device(x, mod(y + 1, NY), z, c), device(x, mod(y - 1, NY), z, c)
    y_far = device(x, mod(y + 2, NY), z, c)
    x_peers = [device(mod(x + i, NX), y, z, c) for i in (1, 2, 3)]

    barrier = pltpu.get_barrier_semaphore()
    peers = [sibling, z_next, z_prev, y_next, y_prev, y_far] + x_peers
    for peer in peers:
        pl.semaphore_signal(barrier, inc=1, device_id=peer, device_id_type=MESH)
    pl.semaphore_wait(barrier, len(peers))

    def part(yy, cc):
        return pl.ds(pl.multiple_of((cc * NY + yy) * TOK, TOK), TOK)

    def columns(i, width):
        return pl.ds(pl.multiple_of(i * width, width), width)

    mine = part(y, c)

    def kv_copy(i, which, owner):
        peer_x = mod(x + i, NX)
        ref = (k_hbm, v_hbm)[which]
        return pltpu.make_async_remote_copy(
            src_ref=ref.at[:, columns(peer_x, HD)],
            dst_ref=kv.at[z, owner, mine, pl.ds(which * HD, HD)],
            send_sem=ks_sem.at[i, which],
            recv_sem=kr_sem.at[owner, which],
            device_id=x_peers[i - 1],
            device_id_type=MESH,
        )

    def q_copy(i):
        return pltpu.make_async_remote_copy(
            src_ref=q_hbm.at[:, columns(mod(x + i, NX), WIDE)],
            dst_ref=qb.at[x],
            send_sem=qs_sem.at[i],
            recv_sem=qr_sem.at[x],
            device_id=x_peers[i - 1],
            device_id_type=MESH,
        )

    def q_arrival(r):
        return pltpu.make_async_remote_copy(
            src_ref=qb.at[r], dst_ref=qb.at[r], send_sem=qs_sem.at[0], recv_sem=qr_sem.at[r],
            device_id=sibling, device_id_type=MESH,
        )

    def o_copy(r, owner):
        return pltpu.make_async_remote_copy(
            src_ref=ob.at[r],
            dst_ref=o_hbm.at[:, columns(owner, WIDE)],
            send_sem=os_sem.at[r],
            recv_sem=or_sem.at[owner],
            device_id=device(r, y, z, c),
            device_id_type=MESH,
        )

    own_k = pltpu.make_async_copy(
        k_hbm.at[:, columns(x, HD)], kv.at[z, x, mine, pl.ds(0, HD)], own_sem.at[0])
    own_v = pltpu.make_async_copy(
        v_hbm.at[:, columns(x, HD)], kv.at[z, x, mine, pl.ds(HD, HD)], own_sem.at[1])
    own_q = pltpu.make_async_copy(q_hbm.at[:, columns(x, WIDE)], qb.at[x], own_sem.at[2])
    own_o = pltpu.make_async_copy(ob.at[x], o_hbm.at[:, columns(x, WIDE)], own_sem.at[3])

    def piece(zz, yy, cc, peer, send):
        ref = kv.at[zz, :, part(yy, cc), :]
        return pltpu.make_async_remote_copy(
            src_ref=ref, dst_ref=ref, send_sem=send, recv_sem=piece_recv.at[zz, yy, cc],
            device_id=peer, device_id_type=MESH,
        )

    def half(zz, n, cc):
        ref = kv.at[zz, :, pl.ds(pl.multiple_of(cc * NY * TOK, NY * TOK), NY * TOK), :]
        return pltpu.make_async_remote_copy(
            src_ref=ref, dst_ref=ref, send_sem=sib_send.at[n, 0], recv_sem=sib_recv.at[n],
            device_id=sibling, device_id_type=MESH,
        )

    def to_sibling(n, k, cc, act):
        zz = place(n)[0]
        def one():
            act(piece(zz, mod(y + offset(k), NY), cc, sibling, sib_send.at[0, k]))
        pl.when(n == 0)(one)
        pl.when((n > 0) & (k == NY - 1))(lambda: act(half(zz, n, cc)))

    def await_sibling(n):
        def pieces():
            for k in range(NY):
                await_piece(0, k, 1 - c)
        pl.when(n == 0)(pieces)
        pl.when(n > 0)(lambda: half(place(n)[0], n, 1 - c).wait_recv())

    def place(n):
        return mod(z + offset(n), NZ), (n + 1) // 2, lax.rem(n, 2) == 1

    def sends0(n, k, act):
        zz, far, up = place(n)
        def to(peer, sem):
            act(piece(zz, mod(y + offset(k), NY), 0, peer, sem))
        to_sibling(n, k, 0, act)
        to_next = (n == 0) | (up & ((far < 3) | ((far == 3) & (k < 2))))
        to_prev = (n == 0) | (~up & ((far < 3) | ((far == 3) & (k >= 2))))
        pl.when(to_next)(lambda: to(z_next, ring_send.at[n, k, 0]))
        pl.when(to_prev)(lambda: to(z_prev, ring_send.at[n, k, 1]))

    def sends1(n, k, act):
        zz, far, up = place(n)
        def to(peer, sem):
            act(piece(zz, mod(y + offset(k), NY), 1, peer, sem))
        to_sibling(n, k, 1, act)
        if k == 0:
            even = lax.rem(y, 2) == 0
            to_next = (n == 0) | (up & ((far < 3) | ((far == 3) & even)))
            to_prev = (n == 0) | (~up & ((far < 3) | ((far == 3) & ~even)))
            pl.when(to_next)(lambda: to(z_next, ring_send.at[n, 3, 0]))
            pl.when(to_prev)(lambda: to(z_prev, ring_send.at[n, 3, 1]))

    def along_y(n, cc, act):
        for i, peer in enumerate((y_next, y_prev, y_far)):
            act(piece(place(n)[0], y, cc, peer, aux_send.at[n, i]))

    def await_piece(n, k, cc):
        yy = mod(y + offset(k), NY)
        piece(place(n)[0], yy, cc, sibling, sib_send.at[n, k]).wait_recv()

    def start(copy):
        copy.start()

    def sent(copy):
        copy.wait_send()

    def serve0(n, k):
        await_piece(n, k, 0)
        sends0(n, k, start)

    def relay1(n, k):
        await_piece(n, k, 1)
        to_sibling(n, k, 1, start)

    def serve1(n, k):
        await_piece(n, k, 1)
        sends1(n, k, start)
        if k == 0:
            if n >= HELD:
                along_y(n - HELD, 1, sent)
            along_y(n, 1, start)

    def pair0(d, k):
        serve0(2 * d - 1, k)
        serve0(2 * d, k)

    for i in (1, 2, 3):
        for which in (0, 1):
            kv_copy(i, which, x).start()
    own_k.start()
    own_v.start()
    for i in (1, 3):
        q_copy(i).start()
    own_q.start()
    own_k.wait()
    own_v.wait()
    for i in (1, 2, 3):
        for which in (0, 1):
            kv_copy(i, which, mod(x - i, NX)).wait_recv()

    @pl.when(c == 0)
    def _():
        sends0(0, 0, start)
        along_y(0, 0, start)

    @pl.when(c == 1)
    def _():
        sends1(0, 0, start)
        along_y(0, 1, start)

    q_copy(2).start()
    m_ref[...] = jnp.full_like(m_ref, LOW)
    acc[...] = jnp.zeros_like(acc)

    @pl.when(c == 0)
    def _():
        lax.fori_loop(1, NY, lambda k, _: (serve0(0, k), 0)[1], 0)

    @pl.when(c == 1)
    def _():
        lax.fori_loop(1, NY, lambda k, _: (relay1(0, k), 0)[1], 0)
        serve1(1, 0)
        serve1(2, 0)

    def attend(zz, r, diagonal):
        spans = r + 1 if diagonal else r
        if not spans:
            return
        keys = kv[zz, :spans, :, :HD].reshape(spans * SPAN, HD)
        values = kv[zz, :spans, :, HD:].reshape(spans * SPAN, HD)
        values = jnp.concatenate([values, jnp.ones_like(values)], axis=1)
        tiles = [pl.ds(r * ROWS + i * TILE, TILE) for i in range(ROWS // TILE)]
        scores = []
        for i in range(len(tiles)):
            heads = range(i * TILE // TOK, (i + 1) * TILE // TOK)
            query = jnp.concatenate([qb[r, :, g * HD:(g + 1) * HD] for g in heads], axis=0)
            scores.append(lax.dot_general(
                query, keys, (((1,), (1,)), ((), ())), preferred_element_type=jnp.float32))
        old = [m_ref[t, :] for t in tiles]
        sums = [acc[t, :] for t in tiles]
        if diagonal:
            lane = lax.broadcasted_iota(jnp.int32, (TILE, HD), 1)
            row = lax.rem(lax.broadcasted_iota(jnp.int32, (TILE, HD), 0), TOK)
            ahead = lane // TOK * (4 * TOK) + lax.rem(lane, TOK) - row
            span_gap = (zh - zz // 2) * (2 * SPAN) + head * TOK - lax.rem(zz, 2) * 2 * TOK
        done = []
        for score, peak, total in zip(scores, old, sums):
            cols = [score[:, j * HD:(j + 1) * HD] for j in range(spans * SPAN // HD)]
            if diagonal:
                for j in range(SPAN // HD):
                    at = len(cols) - SPAN // HD + j
                    cols[at] = jnp.where(
                        ahead <= span_gap - (j % 2 * 8 + j // 2) * TOK, cols[at], LOW)
            top = cols
            while len(top) > 1:
                rest = top[len(top) // 2 * 2:]
                top = [jnp.maximum(a, b) for a, b in zip(top[::2], top[1::2])] + rest
            top = jnp.maximum(peak, jnp.max(top[0], axis=1, keepdims=True))
            factor = jnp.exp2((peak - top) * SCALE)
            weights = jnp.concatenate(
                [jnp.exp2((col - top) * SCALE).astype(jnp.bfloat16) for col in cols], axis=1)
            added = jnp.dot(weights, values, preferred_element_type=jnp.float32)
            total = jnp.concatenate([total[:, :HD] * factor, total[:, HD:] * factor], axis=1)
            done.append((total + added, top))
        for t, (total, top) in zip(tiles, done):
            acc[t, :] = total
            m_ref[t, :] = top

    def finish(r):
        for g in range(GROUP):
            rows = pl.ds(pl.multiple_of(r * ROWS + g * TOK, TOK), TOK)
            out = acc[rows, :HD] / acc[rows, HD:]
            ob[r, :, g * HD:(g + 1) * HD] = out.astype(jnp.bfloat16)

    def work(w, _):
        last = w >= 4 * (NZ - 2)
        slot = jnp.where(last, (w - 4 * (NZ - 2)) // 2, lax.rem(w, 4))
        n = jnp.where(last, NZ - 2 + lax.rem(w, 2), w // 4)
        near = slot + jnp.where(slot == 2, 1, 0) - jnp.where(slot == 3, 1, 0)
        turn = lax.rem(x + jnp.where(last, slot + 1, near), NX)
        r = jnp.where(last | (n == 0), turn, 3 - slot)
        zz = mod(z + offset(n), NZ)

        @pl.when(jnp.where(last, w < 4 * (NZ - 2) + 2, slot == 0))
        def _():
            await_sibling(n)

        @pl.when((c == 0) & (n < 6))
        def _():
            @pl.when((n == 0) & (slot > 0))
            def _():
                pair0(1, slot - 1)
                pl.when(slot == 3)(lambda: pair0(1, 3))

            @pl.when((n > 0) & (n < 5))
            def _():
                far = (n - 1) // 2 + 2
                serve0(2 * far - 1 + lax.rem(slot, 2), 2 * lax.rem(n + 1, 2) + slot // 2)

            @pl.when((n == 5) & (slot > 1))
            def _():
                serve0(7, slot - 2)
                serve0(7, slot)

        @pl.when((c == 1) & (n < 6))
        def _():
            for at, at_slot, m in ((0, 2, 3), (0, 3, 4), (1, 1, 5), (1, 2, 6), (2, 1, 7)):
                pl.when((n == at) & (slot == at_slot))(lambda: serve1(m, 0))
            pl.when(slot > 0)(lambda: relay1(n + 1, slot))

            @pl.when((n == 5) & (slot == 3))
            def _():
                lax.fori_loop(1, NY, lambda k, _: (relay1(7, k), 0)[1], 0)

        @pl.when(n == 0)
        def _():
            pl.when(r == x)(own_q.wait)
            pl.when(r != x)(lambda: q_arrival(r).wait_recv())

        for quarter in range(NX):
            inside = zz // 2 <= zh
            pl.when((r == quarter) & inside)(lambda: attend(zz, quarter, True))
            pl.when((r == quarter) & ~inside)(lambda: attend(zz, quarter, False))

        @pl.when(last & (lax.rem(w, 2) == 1))
        def _():
            finish(r)
            pl.when(r != x)(lambda: o_copy(r, x).start())
            pl.when(r == x)(own_o.start)
        return 0

    lax.fori_loop(0, 4 * NZ, work, 0)

    for i in (1, 2, 3):
        for which in (0, 1):
            kv_copy(i, which, x).wait_send()
        q_copy(i).wait_send()
    pl.when(c == 0)(lambda: along_y(0, 0, sent))

    @pl.when(c == 1)
    def _():
        for n in range(NZ - HELD, NZ):
            along_y(n, 1, sent)

    def drain(n, _):
        for k in range(4):
            pl.when(c == 0)(lambda: sends0(n, k, sent))
            pl.when(c == 1)(lambda: sends1(n, k, sent))
        return 0

    lax.fori_loop(0, NZ, drain, 0)
    own_o.wait()
    for r in range(NX):
        pl.when(r != x)(lambda: o_copy(r, x).wait_send())
        pl.when(r != x)(lambda: o_copy(r, r).wait_recv())


def shards(queries, keys, values):
    dma = pltpu.SemaphoreType.DMA
    return pl.pallas_call(
        kernel,
        out_shape=jax.ShapeDtypeStruct(queries.shape, jnp.bfloat16),
        in_specs=[pl.BlockSpec(memory_space=pl.ANY)] * 3,
        out_specs=pl.BlockSpec(memory_space=pl.ANY),
        scratch_shapes=[
            pltpu.VMEM((NZ, NX, SPAN, 2 * HD), jnp.bfloat16),
            pltpu.VMEM((NX, TOK, WIDE), jnp.bfloat16),
            pltpu.VMEM((NX, TOK, WIDE), jnp.bfloat16),
            pltpu.VMEM((NX * ROWS, HD), jnp.float32),
            pltpu.VMEM((NX * ROWS, 2 * HD), jnp.float32),
            dma((4,)), dma((4,)), dma((4,)), dma((4, 2)), dma((4, 2)), dma((4,)), dma((4,)),
            dma((NZ, NY, 2)), dma((NZ,)), dma((NZ, 4)), dma((NZ, 4, 2)), dma((NZ, 3)),
        ],
        compiler_params=pltpu.CompilerParams(
            collective_id=0, has_side_effects=True, vmem_limit_bytes=56 << 20),
        cost_estimate=pl.CostEstimate(
            flops=9 << 30, bytes_accessed=2 << 20, transcendentals=17 << 20),
    )(queries, keys, values)


def solution(mesh):
    spec = P(("ctx", "head"), None)
    return jax.shard_map(
        shards, mesh=mesh, in_specs=(spec, spec, spec), out_specs=spec, check_vma=False)
```
